32 devices in a mesh: pb: 4 (over y, x), ka: 8 (over z, core).
Axes of the slice: x: 2, y: 2, z: 4, core: 2. Of those that a mesh axis runs over, the one named last changes fastest.
Arguments:
- feat_first: bfloat16 [8192, 128], P(('pb', 'ka')), may hold values from -16 to 16
- feat_second: bfloat16 [8192, 128], P(('ka', 'pb')), may hold values from -18 to 18
- value_weight: bfloat16 [128, 128], replicated, may hold values from -0.5 to 0.5
- out_weight: bfloat16 [128, 128], replicated, may hold values from -0.5 to 0.5
- conv_weight: bfloat16 [3, 3, 128, 128], replicated, may hold values from -0.1875 to 0.1875
- conv_bias: bfloat16 [128], replicated, may hold values from -3 to 3
Outputs:
- refined: bfloat16 [32, 256, 128], P(('pb', 'ka'))
The draws below stay inside these ranges and needn't reach their ends.
All inputs are finite; a program needn't handle non-finite values.
Results may differ from the reference program's by a relative error of at most 0.0055.
Values may be sent and summed in bfloat16 or wider, within the bound.
A program may use at most 192 MiB of HBM per device.

```python
import jax
import jax.numpy as jnp
from jax import lax

C = 128
WIMG = 256
HIMG = 32
TOKENS = 8192


def draw_features(key):
    base = jax.random.fold_in(key, 7)
    key_a, key_b = jax.random.split(base, 2)
    first = 4.0 * jnp.clip(jax.random.normal(key_a, (TOKENS, C), jnp.float32), -4.0, 4.0)
    second = 3.0 * jnp.clip(jax.random.normal(key_b, (TOKENS, C), jnp.float32), -6.0, 6.0)
    return (first, second)


def draw_feat_first(key, part):
    return draw_features(key)[0].astype(jnp.bfloat16)


def draw_feat_second(key, part):
    return draw_features(key)[1].astype(jnp.bfloat16)


def bell_draw(key, extent, spread, bound, held_as=jnp.bfloat16):
    values = spread * jax.random.normal(key, extent, jnp.float32)
    return jnp.clip(values, min=-bound, max=bound).astype(held_as)


def setup_inputs(seed: int = 0) -> dict:
    arg_keys = jax.random.split(jax.random.key(seed), 7)
    feat_first = draw_feat_first(jax.random.fold_in(arg_keys[6], 71), 0)
    feat_second = draw_feat_second(jax.random.fold_in(arg_keys[6], 71), 0)
    value_weight = bell_draw(arg_keys[2], (C, C), C ** -0.5, 0.5)
    out_weight = bell_draw(arg_keys[3], (C, C), C ** -0.5, 0.5)
    conv_weight = bell_draw(arg_keys[4], (3, 3, C, C), (9 * C) ** -0.5, 0.1875)
    conv_bias = bell_draw(arg_keys[5], (C,), 0.5, 3.0)
    return dict(feat_first=feat_first, feat_second=feat_second, value_weight=value_weight, out_weight=out_weight, conv_weight=conv_weight, conv_bias=conv_bias)


def reference(feat_first, feat_second, value_weight, out_weight, conv_weight, conv_bias):
    score_scale = C ** -0.5
    values = jnp.dot(feat_second, value_weight, preferred_element_type=jnp.float32).astype(jnp.bfloat16)
    block_rows = min(512, TOKENS)
    blocks = feat_first.reshape(TOKENS // block_rows, block_rows, C)

    def attend(query_block):
        scores = jnp.dot(query_block, feat_second.T, preferred_element_type=jnp.float32) * score_scale
        row_peak = jnp.max(scores, axis=1, keepdims=True)
        expo = jnp.exp(scores - row_peak)
        row_mass = jnp.sum(expo, axis=1, keepdims=True)
        weighted = jnp.dot(expo.astype(jnp.bfloat16), values, preferred_element_type=jnp.float32)
        return (weighted / row_mass).astype(jnp.bfloat16)

    message = lax.map(attend, blocks).reshape(TOKENS, C)
    mixed_rows = (feat_first.astype(jnp.float32) + jnp.dot(message, out_weight, preferred_element_type=jnp.float32)).astype(jnp.bfloat16)
    grid_image = mixed_rows.reshape(HIMG, WIMG, C)
    padded = jnp.pad(grid_image, ((1, 1), (1, 1), (0, 0)))
    accum_sum = jnp.zeros((HIMG * WIMG, C), jnp.float32)
    for row_shift in range(3):
        for col_shift in range(3):
            window = padded[row_shift:row_shift + HIMG, col_shift:col_shift + WIMG].reshape(HIMG * WIMG, C)
            accum_sum = accum_sum + jnp.dot(window, conv_weight[row_shift, col_shift], preferred_element_type=jnp.float32)
    conv_out = accum_sum.reshape(HIMG, WIMG, C) + conv_bias.astype(jnp.float32)
    return (grid_image.astype(jnp.float32) + jax.nn.gelu(conv_out)).astype(jnp.bfloat16)
```

```python
import functools
import math

import jax
import jax.numpy as jnp
from jax import lax
from jax.experimental import pallas as pl
from jax.experimental.pallas import tpu as pltpu
from jax.sharding import PartitionSpec as P

WIMG = 256
MESH = pl.DeviceIdType.MESH


def kernel(
    n_pb, n_ka,
    q_ref, k_ref, vw_ref, ow_ref, cw_ref, cb_ref, out_ref,
    keys, peer_q, acc, peak, part_out, part_in, mixed, halo,
    z_send, xy_send, key_recv, one_send, one_recv,
):
    rows, width = q_ref.shape
    n_z = n_ka // 2
    bits = [1 << b for b in range(n_pb.bit_length() - 1)]
    orders = (bits, bits[::-1])
    half = rows // 2
    scale = math.log2(math.e) * width ** -0.5

    pb, ka = lax.axis_index("pb"), lax.axis_index("ka")
    z, core = ka // 2, ka % 2
    partner = (pb, z * 2 + 1 - core)
    line = [(pb, lax.rem(z + n_z - k, n_z) * 2 + core) for k in range(1, n_z)]
    across = {b: (pb + b - 2 * b * (pb // b % 2), ka) for b in bits}
    n_rows = n_pb * n_ka
    row = pb * n_ka + ka
    above, below = lax.rem(row + n_rows - 1, n_rows), lax.rem(row + 1, n_rows)
    above_id, below_id = (above // n_ka, above % n_ka), (below // n_ka, below % n_ka)

    barrier = pltpu.get_barrier_semaphore()
    greeted = [partner, above_id, below_id] + line + list(across.values())
    for device in greeted:
        pl.semaphore_signal(barrier, inc=1, device_id=device, device_id_type=MESH)
    keys[0, 0] = k_ref[...]
    pl.semaphore_wait(barrier, len(greeted))

    started = []

    def send(src, dst, send_sem, recv_sem, device):
        copy = pltpu.make_async_remote_copy(
            src_ref=src, dst_ref=dst, send_sem=send_sem, recv_sem=recv_sem,
            device_id=device, device_id_type=MESH,
        )
        copy.start()
        started.append(copy)
        return copy

    def piece(j, k, f):
        return keys.at[j, k, pl.ds(f * half, half)]

    def hop(j, k, f, bit):
        send(
            piece(j, k, f), piece(j ^ bit, k, f),
            xy_send.at[j ^ bit, k, f], key_recv.at[j ^ bit, k, f], across[bit],
        )

    def arrived(j, k, f):
        ref = piece(j, k, f)
        pltpu.make_async_copy(ref, ref, key_recv.at[j, k, f]).wait()

    def forward(j, k, f):
        last = max([i for i, b in enumerate(orders[f]) if j & b], default=-1)
        for bit in orders[f][last + 1:]:
            hop(j, k, f, bit)

    q_copy = send(q_ref, peer_q, one_send.at[0], one_recv.at[0], partner)
    for f in range(2):
        forward(0, 0, f)
        for k in range(1, n_z):
            send(
                piece(0, 0, f), piece(0, k, f),
                z_send.at[k, f], key_recv.at[0, k, f], line[k - 1],
            )

    def attend(j, side, first):
        queries = (peer_q if side == 0 else q_ref)[...]
        block = keys[j].reshape(n_z * rows, width)
        scores = lax.dot_general(
            queries, block, (((1,), (1,)), ((), ())), preferred_element_type=jnp.float32
        ) * scale
        top = jnp.max(scores, axis=1, keepdims=True)
        if not first:
            top = jnp.maximum(top, peak[side][:, :1])
        weights = jnp.exp2(scores - top).astype(jnp.bfloat16)
        extended = jnp.concatenate([block, jnp.ones_like(block)], axis=1)
        total = jnp.dot(weights, extended, preferred_element_type=jnp.float32)
        if not first:
            total = total + acc[side] * jnp.exp2(peak[side][:, :1] - top)
        acc[side] = total
        peak[side] = jnp.broadcast_to(top, (rows, width))

    def receive(j, k):
        for f in range(2):
            arrived(j, k, f)
            forward(j, k, f)

    for k in range(1, n_z):
        receive(0, k)
    q_copy.wait_recv()
    for j in range(n_pb):
        if j:
            for k in range(n_z):
                receive(j, k)
        attend(j, 0, j == 0)
        if j == n_pb - 1:
            lane = lax.broadcasted_iota(jnp.int32, (rows, width), 1)
            part_out[:, :width] = acc[0, :, :width]
            part_out[:, width:] = jnp.where(lane < width // 2, acc[0, :, width:], peak[0])
            part_copy = send(part_out, part_in, one_send.at[1], one_recv.at[1], partner)
        attend(j, 1, j == 0)

    part_copy.wait_recv()
    other_peak = part_in[:, width + width // 2:width + width // 2 + 1]
    other_mass = part_in[:, width:width + 1]
    own_peak = peak[1][:, :1]
    top = jnp.maximum(own_peak, other_peak)
    own_factor, other_factor = jnp.exp2(own_peak - top), jnp.exp2(other_peak - top)
    mass = acc[1, :, width:width + 1] * own_factor + other_mass * other_factor
    blend = (acc[1, :, :width] * own_factor + part_in[:, :width] * other_factor) / mass
    message = jnp.dot(
        blend.astype(jnp.bfloat16), vw_ref[...], preferred_element_type=jnp.float32
    ).astype(jnp.bfloat16)
    mixed[...] = (
        q_ref[...].astype(jnp.float32)
        + jnp.dot(message, ow_ref[...], preferred_element_type=jnp.float32)
    ).astype(jnp.bfloat16)
    down = send(mixed, halo.at[0], one_send.at[2], one_recv.at[2], below_id)
    up = send(mixed, halo.at[1], one_send.at[3], one_recv.at[3], above_id)

    def taps(image, a):
        return [
            jnp.dot(image, cw_ref[a, b], preferred_element_type=jnp.float32) for b in range(3)
        ]

    own = taps(mixed[...], 1)
    down.wait_recv()
    up.wait_recv()
    upper = jnp.where(row > 0, halo[0], jnp.zeros_like(halo[0]))
    lower = jnp.where(row < n_rows - 1, halo[1], jnp.zeros_like(halo[1]))
    left, centre, right = [
        x + y + w for x, y, w in zip(own, taps(upper, 0), taps(lower, 2))
    ]
    column = lax.broadcasted_iota(jnp.int32, (rows, width), 0)
    conv = (
        centre
        + jnp.where(column > 0, pltpu.roll(left, 1, 0), 0.0)
        + jnp.where(column < rows - 1, pltpu.roll(right, rows - 1, 0), 0.0)
        + cb_ref[...].astype(jnp.float32)
    )
    out_ref[...] = (mixed[...].astype(jnp.float32) + jax.nn.gelu(conv)).astype(jnp.bfloat16)
    for copy in started:
        copy.wait_send()


def solution(mesh):
    n_pb, n_ka = mesh.shape["pb"], mesh.shape["ka"]

    def local(feat_first, feat_second, value_weight, out_weight, conv_weight, conv_bias):
        rows, width = feat_first.shape
        assert rows == WIMG and n_ka % 2 == 0 and n_pb & (n_pb - 1) == 0
        n_z = n_ka // 2
        vmem = pl.BlockSpec(memory_space=pltpu.VMEM)
        dma = pltpu.SemaphoreType.DMA
        out = pl.pallas_call(
            functools.partial(kernel, n_pb, n_ka),
            out_shape=jax.ShapeDtypeStruct((rows, width), jnp.bfloat16),
            in_specs=[vmem] * 6,
            out_specs=vmem,
            scratch_shapes=[
                pltpu.VMEM((n_pb, n_z, rows, width), jnp.bfloat16),
                pltpu.VMEM((rows, width), jnp.bfloat16),
                pltpu.VMEM((2, rows, 2 * width), jnp.float32),
                pltpu.VMEM((2, rows, width), jnp.float32),
                pltpu.VMEM((rows, 2 * width), jnp.float32),
                pltpu.VMEM((rows, 2 * width), jnp.float32),
                pltpu.VMEM((rows, width), jnp.bfloat16),
                pltpu.VMEM((2, rows, width), jnp.bfloat16),
                dma((n_z, 2)),
                dma((n_pb, n_z, 2)),
                dma((n_pb, n_z, 2)),
                dma((4,)),
                dma((4,)),
            ],
            compiler_params=pltpu.CompilerParams(
                collective_id=0, has_side_effects=True, vmem_limit_bytes=48 * 1024 * 1024
            ),
        )(feat_first, feat_second, value_weight, out_weight, conv_weight, conv_bias.reshape(1, width))
        return out.reshape(rows // WIMG, WIMG, width)

    in_specs = (P(("pb", "ka"), None), P(("ka", "pb"), None), P(), P(), P(), P())
    out_specs = P(("pb", "ka"), None, None)
    return jax.shard_map(local, mesh=mesh, in_specs=in_specs, out_specs=out_specs, check_vma=False)
```

```python
import functools
import math

import jax
import jax.numpy as jnp
from jax import lax
from jax.experimental import pallas as pl
from jax.experimental.pallas import tpu as pltpu
from jax.sharding import PartitionSpec as P

WIMG = 256
MESH = pl.DeviceIdType.MESH


def kernel(
    n_pb, n_ka,
    q_hbm, k_hbm, vw_hbm, ow_hbm, cw_hbm, cb_hbm, out_ref,
    q_ref, vw_ref, ow_ref, cw_ref, cb_ref,
    keys, peer_q, acc, peak, part_out, part_in, mixed, halo,
    local_sem, z_send, xy_send, key_recv, one_send, one_recv,
):
    rows, width = q_ref.shape
    n_z = n_ka // 2
    bits = [1 << b for b in range(n_pb.bit_length() - 1)]
    orders = (bits, bits[::-1])
    half = rows // 2
    scale = math.log2(math.e) * width ** -0.5

    pb, ka = lax.axis_index("pb"), lax.axis_index("ka")
    z, core = ka // 2, ka % 2
    partner = (pb, z * 2 + 1 - core)
    line = [(pb, lax.rem(z + n_z - k, n_z) * 2 + core) for k in range(1, n_z)]
    across = {b: (pb + b - 2 * b * (pb // b % 2), ka) for b in bits}
    n_rows = n_pb * n_ka
    row = pb * n_ka + ka
    above, below = lax.rem(row + n_rows - 1, n_rows), lax.rem(row + 1, n_rows)
    above_id, below_id = (above // n_ka, above % n_ka), (below // n_ka, below % n_ka)

    barrier = pltpu.get_barrier_semaphore()
    greeted = [partner, above_id, below_id] + line + list(across.values())
    for device in greeted:
        pl.semaphore_signal(barrier, inc=1, device_id=device, device_id_type=MESH)
    fetches = [
        pltpu.make_async_copy(src, dst, local_sem.at[i])
        for i, (src, dst) in enumerate((
            (k_hbm, keys.at[0, 0]), (q_hbm, q_ref), (vw_hbm, vw_ref),
            (ow_hbm, ow_ref), (cw_hbm, cw_ref), (cb_hbm, cb_ref),
        ))
    ]
    for fetch in fetches:
        fetch.start()
    pl.semaphore_wait(barrier, len(greeted))

    started = []

    def send(src, dst, send_sem, recv_sem, device):
        copy = pltpu.make_async_remote_copy(
            src_ref=src, dst_ref=dst, send_sem=send_sem, recv_sem=recv_sem,
            device_id=device, device_id_type=MESH,
        )
        copy.start()
        started.append(copy)
        return copy

    def piece(j, k, f):
        return keys.at[j, k, pl.ds(f * half, half)]

    def source(j, k, f):
        return piece(j, k, f) if j or k else k_hbm.at[pl.ds(f * half, half)]

    def hop(j, k, f, bit):
        send(
            source(j, k, f), piece(j ^ bit, k, f),
            xy_send.at[j ^ bit, k, f], key_recv.at[j ^ bit, k, f], across[bit],
        )

    def arrived(j, k, f):
        ref = piece(j, k, f)
        pltpu.make_async_copy(ref, ref, key_recv.at[j, k, f]).wait()

    def onward(j, f):
        last = max([i for i, b in enumerate(orders[f]) if j & b], default=-1)
        return orders[f][last + 1:]

    def forward(j, k, f):
        for bit in onward(j, f):
            hop(j, k, f, bit)

    def receive(j, k, f):
        arrived(j, k, f)
        forward(j, k, f)

    def queries_of(side):
        return peer_q if side == 0 else q_ref

    def attend(j, k0, k1, side, first=False):
        block = keys[j, k0:k1].reshape((k1 - k0) * rows, width)
        scores = lax.dot_general(
            queries_of(side)[...], block, (((1,), (1,)), ((), ())),
            preferred_element_type=jnp.float32,
        ) * scale
        top = jnp.max(scores, axis=1, keepdims=True)
        if not first:
            top = jnp.maximum(top, peak[side][:, :1])
        weights = jnp.exp2(scores - top).astype(jnp.bfloat16)
        extended = jnp.concatenate([block, jnp.ones_like(block)], axis=1)
        total = jnp.dot(weights, extended, preferred_element_type=jnp.float32)
        if not first:
            total = total + acc[side] * jnp.exp2(peak[side][:, :1] - top)
        acc[side] = total
        peak[side] = jnp.broadcast_to(top, (rows, width))

    for f in range(2):
        forward(0, 0, f)
        for k in range(1, n_z):
            send(
                source(0, 0, f), piece(0, k, f),
                z_send.at[k, f], key_recv.at[0, k, f], line[k - 1],
            )
    q_copy = send(q_hbm, peer_q, one_send.at[0], one_recv.at[0], partner)
    fetches[0].wait()
    fetches[1].wait()

    relayed = sorted(
        (bin(j).count("1"), j, f)
        for f in range(2) for j in range(1, n_pb) if onward(j, f)
    )
    halfway = (n_z + 1) // 2

    def relay(k):
        for _, j, f in relayed:
            receive(j, k, f)

    for k in range(1, n_z):
        for f in range(2):
            receive(0, k, f)
        relay(k - 1)
        if k == 1:
            q_copy.wait_recv()
        if k == halfway:
            for side in range(2):
                attend(0, 0, halfway, side, first=True)
    relay(n_z - 1)
    for side in range(2):
        attend(0, halfway, n_z, side)
    for j in range(1, n_pb):
        last = j == n_pb - 1
        parts = ((0, halfway), (halfway, n_z)) if last else ((0, n_z),)
        for k0, k1 in parts:
            for k in range(k0, k1):
                for f in range(2):
                    if not onward(j, f):
                        arrived(j, k, f)
            attend(j, k0, k1, 0)
            if last and k1 == n_z:
                lane = lax.broadcasted_iota(jnp.int32, (rows, width), 1)
                part_out[:, :width] = acc[0, :, :width]
                part_out[:, width:] = jnp.where(lane < width // 2, acc[0, :, width:], peak[0])
                part_copy = send(part_out, part_in, one_send.at[1], one_recv.at[1], partner)
            attend(j, k0, k1, 1)

    for fetch in fetches[2:]:
        fetch.wait()
    part_copy.wait_recv()
    other_peak = part_in[:, width + width // 2:width + width // 2 + 1]
    other_mass = part_in[:, width:width + 1]
    own_peak = peak[1][:, :1]
    top = jnp.maximum(own_peak, other_peak)
    own_factor, other_factor = jnp.exp2(own_peak - top), jnp.exp2(other_peak - top)
    mass = acc[1, :, width:width + 1] * own_factor + other_mass * other_factor
    blend = (acc[1, :, :width] * own_factor + part_in[:, :width] * other_factor) / mass
    message = jnp.dot(
        blend.astype(jnp.bfloat16), vw_ref[...], preferred_element_type=jnp.float32
    ).astype(jnp.bfloat16)
    mixed[...] = (
        q_ref[...].astype(jnp.float32)
        + jnp.dot(message, ow_ref[...], preferred_element_type=jnp.float32)
    ).astype(jnp.bfloat16)
    down = send(mixed, halo.at[0], one_send.at[2], one_recv.at[2], below_id)
    up = send(mixed, halo.at[1], one_send.at[3], one_recv.at[3], above_id)

    def taps(image, a):
        return [
            jnp.dot(image, cw_ref[a, b], preferred_element_type=jnp.float32) for b in range(3)
        ]

    own = taps(mixed[...], 1)
    down.wait_recv()
    up.wait_recv()
    upper = jnp.where(row > 0, halo[0], jnp.zeros_like(halo[0]))
    lower = jnp.where(row < n_rows - 1, halo[1], jnp.zeros_like(halo[1]))
    left, centre, right = [
        x + y + w for x, y, w in zip(own, taps(upper, 0), taps(lower, 2))
    ]
    column = lax.broadcasted_iota(jnp.int32, (rows, width), 0)
    conv = (
        centre
        + jnp.where(column > 0, pltpu.roll(left, 1, 0), 0.0)
        + jnp.where(column < rows - 1, pltpu.roll(right, rows - 1, 0), 0.0)
        + cb_ref[...].astype(jnp.float32)
    )
    out_ref[...] = (mixed[...].astype(jnp.float32) + jax.nn.gelu(conv)).astype(jnp.bfloat16)
    for copy in started:
        copy.wait_send()


def solution(mesh):
    n_pb, n_ka = mesh.shape["pb"], mesh.shape["ka"]

    def local(feat_first, feat_second, value_weight, out_weight, conv_weight, conv_bias):
        rows, width = feat_first.shape
        assert rows == WIMG and n_ka % 2 == 0 and n_pb & (n_pb - 1) == 0
        n_z = n_ka // 2
        vmem = pl.BlockSpec(memory_space=pltpu.VMEM)
        dma = pltpu.SemaphoreType.DMA
        out = pl.pallas_call(
            functools.partial(kernel, n_pb, n_ka),
            out_shape=jax.ShapeDtypeStruct((rows, width), jnp.bfloat16),
            in_specs=[pl.BlockSpec(memory_space=pl.ANY)] * 6,
            out_specs=vmem,
            scratch_shapes=[
                pltpu.VMEM((rows, width), jnp.bfloat16),
                pltpu.VMEM(value_weight.shape, jnp.bfloat16),
                pltpu.VMEM(out_weight.shape, jnp.bfloat16),
                pltpu.VMEM(conv_weight.shape, jnp.bfloat16),
                pltpu.VMEM((1, width), jnp.bfloat16),
                pltpu.VMEM((n_pb, n_z, rows, width), jnp.bfloat16),
                pltpu.VMEM((rows, width), jnp.bfloat16),
                pltpu.VMEM((2, rows, 2 * width), jnp.float32),
                pltpu.VMEM((2, rows, width), jnp.float32),
                pltpu.VMEM((rows, 2 * width), jnp.float32),
                pltpu.VMEM((rows, 2 * width), jnp.float32),
                pltpu.VMEM((rows, width), jnp.bfloat16),
                pltpu.VMEM((2, rows, width), jnp.bfloat16),
                dma((6,)),
                dma((n_z, 2)),
                dma((n_pb, n_z, 2)),
                dma((n_pb, n_z, 2)),
                dma((4,)),
                dma((4,)),
            ],
            compiler_params=pltpu.CompilerParams(
                collective_id=0, has_side_effects=True, vmem_limit_bytes=60 * 1024 * 1024
            ),
        )(feat_first, feat_second, value_weight, out_weight, conv_weight, conv_bias.reshape(1, width))
        return out.reshape(rows // WIMG, WIMG, width)

    in_specs = (P(("pb", "ka"), None), P(("ka", "pb"), None), P(), P(), P(), P())
    out_specs = P(("pb", "ka"), None, None)
    return jax.shard_map(local, mesh=mesh, in_specs=in_specs, out_specs=out_specs, check_vma=False)
```

```python
import functools
import math

import jax
import jax.numpy as jnp
from jax import lax
from jax.experimental import pallas as pl
from jax.experimental.pallas import tpu as pltpu
from jax.sharding import PartitionSpec as P

WIMG = 256
MESH = pl.DeviceIdType.MESH


def kernel(
    n_pb, n_ka,
    q_hbm, k_hbm, vw_hbm, ow_hbm, cw_hbm, cb_hbm, out_ref,
    q_ref, vw_ref, ow_ref, cw_ref, cb_ref,
    keys, peer_q, acc, peak, part_out, part_in, mixed, halo,
    local_sem, z_send, xy_send, key_recv, one_send, one_recv,
):
    rows, width = q_ref.shape
    n_z = n_ka // 2
    bits = [1 << b for b in range(n_pb.bit_length() - 1)]
    orders = (bits, bits[::-1])
    half = rows // 2
    scale = math.log2(math.e) * width ** -0.5

    pb, ka = lax.axis_index("pb"), lax.axis_index("ka")
    z, core = ka // 2, ka % 2
    partner = (pb, z * 2 + 1 - core)
    line = [(pb, lax.rem(z + n_z + step, n_z) * 2 + core) for step in (-1, 1)]
    nearest = [
        sorted(range(n_z), key=lambda other: (abs(other - i), i - other)) for i in range(n_z)
    ]
    across = {b: (pb + b - 2 * b * (pb // b % 2), ka) for b in bits}
    n_rows = n_pb * n_ka
    row = pb * n_ka + ka
    above, below = lax.rem(row + n_rows - 1, n_rows), lax.rem(row + 1, n_rows)
    above_id, below_id = (above // n_ka, above % n_ka), (below // n_ka, below % n_ka)

    barrier = pltpu.get_barrier_semaphore()
    greeted = [partner, above_id, below_id] + line + list(across.values())
    for device in greeted:
        pl.semaphore_signal(barrier, inc=1, device_id=device, device_id_type=MESH)
    fetches = [
        pltpu.make_async_copy(src, dst, local_sem.at[i])
        for i, (src, dst) in enumerate((
            (k_hbm, keys.at[0, 0]), (q_hbm, q_ref), (vw_hbm, vw_ref),
            (ow_hbm, ow_ref), (cw_hbm, cw_ref), (cb_hbm, cb_ref),
        ))
    ]
    for fetch in fetches:
        fetch.start()
    pl.semaphore_wait(barrier, len(greeted))

    started = []

    def send(src, dst, send_sem, recv_sem, device):
        copy = pltpu.make_async_remote_copy(
            src_ref=src, dst_ref=dst, send_sem=send_sem, recv_sem=recv_sem,
            device_id=device, device_id_type=MESH,
        )
        copy.start()
        started.append(copy)
        return copy

    def piece(j, k, f):
        return keys.at[j, k, pl.ds(f * half, half)]

    def source(j, k, f):
        return piece(j, k, f) if j or k else k_hbm.at[pl.ds(f * half, half)]

    def hop(j, k, f, bit):
        send(
            source(j, k, f), piece(j ^ bit, k, f),
            xy_send.at[j ^ bit, k, f], key_recv.at[j ^ bit, k, f], across[bit],
        )

    def arrived(j, k, f):
        ref = piece(j, k, f)
        pltpu.make_async_copy(ref, ref, key_recv.at[j, k, f]).wait()

    def onward(j, f):
        last = max([i for i, b in enumerate(orders[f]) if j & b], default=-1)
        return orders[f][last + 1:]

    def forward(j, k, f):
        for bit in onward(j, f):
            hop(j, k, f, bit)

    def receive(j, k, f):
        arrived(j, k, f)
        forward(j, k, f)

    def queries_of(side):
        return peer_q if side == 0 else q_ref

    def attend(j, k0, k1, side, first=False):
        block = keys[j, k0:k1].reshape((k1 - k0) * rows, width)
        scores = lax.dot_general(
            queries_of(side)[...], block, (((1,), (1,)), ((), ())),
            preferred_element_type=jnp.float32,
        ) * scale
        top = jnp.max(scores, axis=1, keepdims=True)
        if not first:
            top = jnp.maximum(top, peak[side][:, :1])
        weights = jnp.exp2(scores - top).astype(jnp.bfloat16)
        extended = jnp.concatenate([block, jnp.ones_like(block)], axis=1)
        total = jnp.dot(weights, extended, preferred_element_type=jnp.float32)
        if not first:
            total = total + acc[side] * jnp.exp2(peak[side][:, :1] - top)
        acc[side] = total
        peak[side] = jnp.broadcast_to(top, (rows, width))

    def z_copy(k, f, here, there, sem):
        return pltpu.make_async_remote_copy(
            src_ref=source(0, k, f),
            dst_ref=piece(0, nearest[there].index(nearest[here][k]), f),
            send_sem=z_send.at[sem, f],
            recv_sem=key_recv.at[0, nearest[there].index(nearest[here][k]), f],
            device_id=(pb, there * 2 + core),
            device_id_type=MESH,
        )

    def z_hops(k, here):
        owner = nearest[here][k]
        return [
            (k if there < here else n_z + k, there)
            for there in (here - 1, here + 1)
            if 0 <= there < n_z and (owner - here) * (there - here) <= 0
        ]

    def each_place(act):
        for here in range(n_z):
            pl.when(z == here)(functools.partial(act, here))

    def z_forward(k, here):
        for sem, there in z_hops(k, here):
            for f in range(2):
                z_copy(k, f, here, there, sem).start()

    def z_drain(here):
        for k in range(n_z):
            for sem, there in z_hops(k, here):
                for f in range(2):
                    z_copy(k, f, here, there, sem).wait_send()

    each_place(functools.partial(z_forward, 0))
    for f in range(2):
        forward(0, 0, f)
    q_copy = send(q_hbm, peer_q, one_send.at[0], one_recv.at[0], partner)
    fetches[0].wait()
    fetches[1].wait()

    relayed = sorted(
        (bin(j).count("1"), j, f)
        for f in range(2) for j in range(1, n_pb) if onward(j, f)
    )
    halfway = (n_z + 1) // 2

    def relay(k):
        for _, j, f in relayed:
            receive(j, k, f)

    for k in range(1, n_z):
        for f in range(2):
            arrived(0, k, f)
        each_place(functools.partial(z_forward, k))
        for f in range(2):
            forward(0, k, f)
        relay(k - 1)
        if k == 1:
            q_copy.wait_recv()
        if k == halfway:
            for side in range(2):
                attend(0, 0, halfway, side, first=True)
    relay(n_z - 1)
    for side in range(2):
        attend(0, halfway, n_z, side)
    for j in range(1, n_pb):
        last = j == n_pb - 1
        parts = ((0, halfway), (halfway, n_z)) if last else ((0, n_z),)
        for k0, k1 in parts:
            for k in range(k0, k1):
                for f in range(2):
                    if not onward(j, f):
                        arrived(j, k, f)
            attend(j, k0, k1, 0)
            if last and k1 == n_z:
                lane = lax.broadcasted_iota(jnp.int32, (rows, width), 1)
                part_out[:, :width] = acc[0, :, :width]
                part_out[:, width:] = jnp.where(lane < width // 2, acc[0, :, width:], peak[0])
                part_copy = send(part_out, part_in, one_send.at[1], one_recv.at[1], partner)
            attend(j, k0, k1, 1)

    for fetch in fetches[2:]:
        fetch.wait()
    part_copy.wait_recv()
    other_peak = part_in[:, width + width // 2:width + width // 2 + 1]
    other_mass = part_in[:, width:width + 1]
    own_peak = peak[1][:, :1]
    top = jnp.maximum(own_peak, other_peak)
    own_factor, other_factor = jnp.exp2(own_peak - top), jnp.exp2(other_peak - top)
    mass = acc[1, :, width:width + 1] * own_factor + other_mass * other_factor
    blend = (acc[1, :, :width] * own_factor + part_in[:, :width] * other_factor) / mass
    message = jnp.dot(
        blend.astype(jnp.bfloat16), vw_ref[...], preferred_element_type=jnp.float32
    ).astype(jnp.bfloat16)
    mixed[...] = (
        q_ref[...].astype(jnp.float32)
        + jnp.dot(message, ow_ref[...], preferred_element_type=jnp.float32)
    ).astype(jnp.bfloat16)
    down = send(mixed, halo.at[0], one_send.at[2], one_recv.at[2], below_id)
    up = send(mixed, halo.at[1], one_send.at[3], one_recv.at[3], above_id)

    def taps(image, a):
        return [
            jnp.dot(image, cw_ref[a, b], preferred_element_type=jnp.float32) for b in range(3)
        ]

    own = taps(mixed[...], 1)
    down.wait_recv()
    up.wait_recv()
    upper = jnp.where(row > 0, halo[0], jnp.zeros_like(halo[0]))
    lower = jnp.where(row < n_rows - 1, halo[1], jnp.zeros_like(halo[1]))
    left, centre, right = [
        x + y + w for x, y, w in zip(own, taps(upper, 0), taps(lower, 2))
    ]
    column = lax.broadcasted_iota(jnp.int32, (rows, width), 0)
    conv = (
        centre
        + jnp.where(column > 0, pltpu.roll(left, 1, 0), 0.0)
        + jnp.where(column < rows - 1, pltpu.roll(right, rows - 1, 0), 0.0)
        + cb_ref[...].astype(jnp.float32)
    )
    out_ref[...] = (mixed[...].astype(jnp.float32) + jax.nn.gelu(conv)).astype(jnp.bfloat16)
    for copy in started:
        copy.wait_send()
    each_place(z_drain)


def solution(mesh):
    n_pb, n_ka = mesh.shape["pb"], mesh.shape["ka"]

    def local(feat_first, feat_second, value_weight, out_weight, conv_weight, conv_bias):
        rows, width = feat_first.shape
        assert rows == WIMG and n_ka % 2 == 0 and n_pb & (n_pb - 1) == 0
        n_z = n_ka // 2
        vmem = pl.BlockSpec(memory_space=pltpu.VMEM)
        dma = pltpu.SemaphoreType.DMA
        out = pl.pallas_call(
            functools.partial(kernel, n_pb, n_ka),
            out_shape=jax.ShapeDtypeStruct((rows, width), jnp.bfloat16),
            in_specs=[pl.BlockSpec(memory_space=pl.ANY)] * 6,
            out_specs=vmem,
            scratch_shapes=[
                pltpu.VMEM((rows, width), jnp.bfloat16),
                pltpu.VMEM(value_weight.shape, jnp.bfloat16),
                pltpu.VMEM(out_weight.shape, jnp.bfloat16),
                pltpu.VMEM(conv_weight.shape, jnp.bfloat16),
                pltpu.VMEM((1, width), jnp.bfloat16),
                pltpu.VMEM((n_pb, n_z, rows, width), jnp.bfloat16),
                pltpu.VMEM((rows, width), jnp.bfloat16),
                pltpu.VMEM((2, rows, 2 * width), jnp.float32),
                pltpu.VMEM((2, rows, width), jnp.float32),
                pltpu.VMEM((rows, 2 * width), jnp.float32),
                pltpu.VMEM((rows, 2 * width), jnp.float32),
                pltpu.VMEM((rows, width), jnp.bfloat16),
                pltpu.VMEM((2, rows, width), jnp.bfloat16),
                dma((6,)),
                dma((2 * n_z, 2)),
                dma((n_pb, n_z, 2)),
                dma((n_pb, n_z, 2)),
                dma((4,)),
                dma((4,)),
            ],
            compiler_params=pltpu.CompilerParams(
                collective_id=0, has_side_effects=True, vmem_limit_bytes=60 * 1024 * 1024
            ),
        )(feat_first, feat_second, value_weight, out_weight, conv_weight, conv_bias.reshape(1, width))
        return out.reshape(rows // WIMG, WIMG, width)

    in_specs = (P(("pb", "ka"), None), P(("ka", "pb"), None), P(), P(), P(), P())
    out_specs = P(("pb", "ka"), None, None)
    return jax.shard_map(local, mesh=mesh, in_specs=in_specs, out_specs=out_specs, check_vma=False)
```
